256 devices in a mesh: dp: 4 (over y), expert: 64 (over z, x, core).
Axes of the slice: x: 4, y: 4, z: 8, core: 2. Of those that a mesh axis runs over, the one named last changes fastest.
Arguments:
- tokens: bfloat16 [16384, 4096], P(('dp', 'expert')), may hold values from -6 to 6
- expert_ids: int32 [16384, 8], P(('dp', 'expert')), may hold values from 0 to 63, all different within a row; in each aligned block of 64 rows (0 to 63, 64 to 127, ...) at most 9 rows name the same one
- gate_values: float32 [16384, 8], P(('dp', 'expert')), may hold values from 0.05 to 0.5
- swap_mask: int32 [32], replicated, may hold values from 0 to 1, as said below
- gate_weight: bfloat16 [64, 4096, 1536], P('expert', None, 'dp'), may hold values from -0.09375 to 0.09375
- up_weight: bfloat16 [64, 4096, 1536], P('expert', None, 'dp'), may hold values from -0.09375 to 0.09375
- down_weight: bfloat16 [64, 1536, 4096], P('expert', 'dp'), may hold values from -0.15625 to 0.15625
Outputs:
- mixed: bfloat16 [16384, 4096], P(('dp', 'expert'))
The draws below stay inside these ranges and needn't reach their ends.
Inputs may be any that keep to these rules, and one draw needn't show every extreme that they name: `expert_ids`: within each aligned block of 64 tokens (the tokens of one device) no slot is chosen more than 9 times, and some slot is chosen exactly 9 times in some block. A token's 8 slots differ. `swap_mask`: at least one pair exchanges and at least one pair does not.
All inputs are finite; a program needn't handle non-finite values.
Results may differ from the reference program's by a relative error of at most 0.015.
Values may be sent and summed in bfloat16 or wider, within the bound.
No kernel may reach another device: no remote copies, remote signals or barrier semaphores. Data moves between devices by JAX's collectives and lax.ppermute only.
A program may use at most 128 MiB of HBM per device.

```python
import math
import jax
import jax.numpy as jnp
import numpy as np
from jax import lax

D = 4096
FF = 1536
TOP = 8
TOK_DEV = 64
EXPERTS = 64
TOKENS = 16384
CAP = 9
N_DP = 4


def draw_swap_mask(key, part):
    key = jax.random.fold_in(key, 5)
    half_size = EXPERTS // 2
    flags = jax.random.randint(jax.random.fold_in(key, 1), (half_size,), 0, 2).astype(jnp.int32)
    pos_off = jax.random.randint(jax.random.fold_in(key, 2), (), 1, half_size - 1).astype(jnp.int32)
    flags = flags.at[0].set(1)
    flags = flags.at[half_size - 1].set(1)
    flags = flags.at[pos_off].set(0)
    return flags


def level_of(key, extent, split, low, top_value):
    gain = 1.0
    for dim, parts in split:
        draws = jax.random.uniform(jax.random.fold_in(jax.random.fold_in(key, 6), dim), (parts,), jnp.float32, low / len(split), top_value / len(split))
        gain = gain * jnp.repeat(jnp.exp(draws), extent[dim] // parts).reshape((-1,) + (1,) * (len(extent) - 1 - dim))
    return gain


def shared_out(rng, own, number, rows, count, top, limit, lean):
    ranking = jax.random.permutation(rng, count)
    heavy_load, common = portions_of(count, rows * top, limit, lean, True), portions_of(count, rows * top, limit, lean, False)
    places = jnp.arange(count)

    def named(lengths, rotation):
        used = int((lengths > 0).sum())
        fixed = max(1, used // 4)
        moved = fixed + (places - fixed + rotation * (used - fixed)) % max(1, count - fixed)
        return jnp.zeros((count,), jnp.int32).at[ranking[jnp.where(places < fixed, places, moved)]].set(jnp.asarray(lengths, jnp.int32))

    lengths = jnp.where(number % 4 == 0, named(heavy_load, number // 4), named(common, number - number // 4 - 1))
    mixed = jax.random.permutation(jax.random.fold_in(own, 3), count)
    giver, taker = mixed[0:count // 2 * 2:2], mixed[1:count // 2 * 2:2]
    slack = jnp.minimum(lengths[giver] - 1, limit - lengths[taker]) // 2
    slack = jnp.where((giver == ranking[0]) | (taker == ranking[0]) | (lengths[taker] == 0), 0, jnp.maximum(slack, 0))
    moved = jax.random.randint(jax.random.fold_in(own, 4), (count // 2,), 0, 1 << 20) % (slack + 1)
    lengths = lengths.at[giver].add(-moved).at[taker].add(moved)
    labels = jnp.searchsorted(jnp.cumsum(lengths), jnp.arange(rows * top), side="right").astype(jnp.int32)
    listing = labels.reshape(top, rows).T
    listing = listing[jax.random.permutation(jax.random.fold_in(own, 1), rows)]
    rotation = jax.random.randint(jax.random.fold_in(own, 2), (rows, 1), 0, top)
    return jnp.take_along_axis(listing, (jnp.arange(top)[None, :] + rotation) % top, axis=1)


def portions_of(count, total, reach, slope, full):
    loads = [(1 << 20) // math.isqrt(rank ** slope) + 1 for rank in range(1, count + 1)]
    largest = reach if full else min(reach, max(-(-total // count), total * loads[0] // sum(loads)))
    least = 1 if total - largest >= count - 1 else 0
    given, surplus = [largest] + [least] * (count - 1), total - largest - least * (count - 1)
    while surplus > 0:
        candidates = [i for i in range(1, count) if given[i] < largest] or [i for i in range(1, count) if given[i] < reach]
        pool, left = sum([loads[i] for i in candidates]), surplus
        for i in candidates:
            more = min(reach - given[i], max(1, left * loads[i] // pool), surplus)
            given[i] = given[i] + more
            surplus = surplus - more
    return np.array(given)


def gaussian(key, dims, deviation, limit, split=(), held_as=jnp.bfloat16):
    result = jax.random.normal(key, dims, jnp.float32) * deviation
    if len(split) > 0:
        result = level_of(key, dims, split, -0.22, 0.18) * result
    return jnp.clip(result, min=-limit, max=limit).astype(held_as)


def setup_inputs(seed: int = 0) -> dict:
    key_of = jax.random.split(jax.random.key(seed), 8)
    tokens = gaussian(key_of[0], (TOKENS, D), 1.0, 6.0, ((0, 256),))
    expert_ids_keys = jax.random.split(jax.random.fold_in(key_of[1], 1), TOKENS // TOK_DEV)
    expert_ids_turns = jax.random.permutation(jax.random.fold_in(key_of[1], 3), TOKENS // TOK_DEV)
    expert_ids = jax.vmap(lambda own, number: shared_out(jax.random.fold_in(key_of[1], 2), own, number, TOK_DEV, EXPERTS, TOP, CAP, 2))(expert_ids_keys, expert_ids_turns).reshape((TOKENS, TOP))
    gate_values = jnp.clip(jnp.exp(math.log(0.5) - 2.3025851 * jax.random.uniform(key_of[2], (TOKENS, TOP), jnp.float32) ** level_of(key_of[2], (TOKENS, TOP), ((0, 256),), -0.2, 0.2)), 0.05, 0.5)
    swap_mask = draw_swap_mask(jax.random.fold_in(key_of[7], 71), 0)
    gate_weight = gaussian(key_of[4], (EXPERTS, D, FF), D ** -0.5, 0.09375, ((0, 64), (2, 4)))
    up_weight = gaussian(key_of[5], (EXPERTS, D, FF), D ** -0.5, 0.09375, ((0, 64), (2, 4)))
    down_weight = gaussian(key_of[6], (EXPERTS, FF, D), FF ** -0.5, 0.15625, ((0, 64), (1, 4)))
    return dict(tokens=tokens, expert_ids=expert_ids, gate_values=gate_values, swap_mask=swap_mask, gate_weight=gate_weight, up_weight=up_weight, down_weight=down_weight)


def reference(tokens, expert_ids, gate_values, swap_mask, gate_weight, up_weight, down_weight):
    expert_count = EXPERTS
    half_size = expert_count // 2
    blocks = TOKENS // TOK_DEV
    capacity = CAP
    slot_iota = jnp.arange(expert_count, dtype=jnp.int32)
    flipped = swap_mask[slot_iota % half_size]
    placement = jnp.where(flipped == 1, jnp.bitwise_xor(slot_iota, half_size), slot_iota).astype(jnp.int32)
    block_ids = expert_ids.reshape(blocks, TOK_DEV * TOP)
    one_hot = (block_ids[:, :, None] == slot_iota[None, None, :]).astype(jnp.int32)
    slot_rank = jnp.sum((jnp.cumsum(one_hot, axis=1) - one_hot) * one_hot, axis=2)
    source = jnp.arange(blocks, dtype=jnp.int32)[:, None]
    column = (source * capacity + slot_rank).reshape(TOKENS, TOP).astype(jnp.int32)
    dispatched = jnp.zeros((expert_count, blocks * capacity, D), jnp.bfloat16)
    for choose in range(TOP):
        dispatched = dispatched.at[expert_ids[:, choose], column[:, choose]].set(tokens)
    quarter_size = FF // N_DP

    def slot_ffn(slot):
        holder = placement[slot]
        slot_rows = dispatched[slot]
        w_gate = gate_weight[holder]
        w_up = up_weight[holder]
        w_down = down_weight[holder]
        total = jnp.zeros((blocks * capacity, D), jnp.float32)
        for quarter in range(N_DP):
            first_col = quarter * quarter_size
            gate_act = jnp.dot(slot_rows, w_gate[:, first_col:first_col + quarter_size], preferred_element_type=jnp.float32)
            up_act = jnp.dot(slot_rows, w_up[:, first_col:first_col + quarter_size], preferred_element_type=jnp.float32)
            hidden = (jax.nn.silu(gate_act) * up_act).astype(jnp.bfloat16)
            partial_value = jnp.dot(hidden, w_down[first_col:first_col + quarter_size, :], preferred_element_type=jnp.float32)
            rounded = lax.optimization_barrier(partial_value.astype(jnp.bfloat16))
            total = total + rounded.astype(jnp.float32)
        return total.astype(jnp.bfloat16)

    results = lax.map(slot_ffn, slot_iota)
    combined = jnp.zeros((TOKENS, D), jnp.float32)
    for choose in range(TOP):
        picked = results[expert_ids[:, choose], column[:, choose]].astype(jnp.float32)
        combined = combined + gate_values[:, choose:choose + 1] * picked
    return combined.astype(jnp.bfloat16)
```

```python
import functools
import jax
import jax.numpy as jnp
from jax import lax
from jax.experimental import pallas as pl
from jax.experimental.pallas import tpu as pltpu
from jax.sharding import Mesh, PartitionSpec as P

Y, Z, X, C = "y", "z", "x", "c"
ALL = (Y, Z, X, C)
XC = (X, C)
N_Y, N_Z, N_XC = 4, 8, 8
EXTRA = 128
VMEM = 48 << 20


def shift(block, axis, by):
    count = lax.axis_size(axis)
    return lax.ppermute(block, axis, [(i, (i + by) % count) for i in range(count)])


def after(value, *others):
    return lax.optimization_barrier((value, *others))[0]


def codes_of(expert_ids, swap_mask, capacity):
    experts = N_Z * N_XC
    slots = jnp.arange(experts, dtype=jnp.int32)
    flipped = swap_mask[slots % (experts // 2)]
    holder = jnp.where(flipped == 1, slots ^ (experts // 2), slots)
    chosen = expert_ids.reshape(-1)
    one_hot = (chosen[:, None] == slots[None, :]).astype(jnp.int32)
    rank = jnp.sum((jnp.cumsum(one_hot, axis=0) - one_hot) * one_hot, axis=1)
    held_by = jnp.sum(one_hot * holder[None, :], axis=1)
    return held_by.reshape(expert_ids.shape), rank.reshape(expert_ids.shape)


def pairs_of(extra, top, capacity):
    values = extra.astype(jnp.float32)
    held_by = values[:, :top].astype(jnp.int32)
    rank = values[:, top : 2 * top].astype(jnp.int32)
    gates = values[:, 2 * top : 3 * top]
    source = jnp.arange(extra.shape[0], dtype=jnp.int32)[:, None] // (extra.shape[0] // N_Z)
    here = held_by // N_XC == lax.axis_index(Z)
    row = (held_by % N_XC * N_Z + source) * capacity + rank
    return jnp.where(here, row, -1), gates


def woven(parts, block):
    if len(parts) == 1:
        return parts[0]
    count = parts[0].shape[0] // block
    return jnp.concatenate([p[i * block : (i + 1) * block] for i in range(count) for p in parts], axis=0)


def unwoven(value, groups, block):
    if groups == 1:
        return [value]
    count = value.shape[0] // (block * groups)
    return [
        jnp.concatenate([value[(i * groups + g) * block : (i * groups + g + 1) * block] for i in range(count)], axis=0)
        for g in range(groups)
    ]


def pick_kernel(groups, per_token, per_row, rows_ref, tokens_ref, out_ref, matrix):
    @pl.when(pl.program_id(0) == 0)
    def _():
        for g in range(groups):
            slot = lax.broadcasted_iota(jnp.int32, matrix.shape[1:], 0)
            hit = jnp.zeros(matrix.shape[1:], jnp.float32)
            for k in range(rows_ref.shape[1]):
                hit = jnp.where(rows_ref[g, k : k + 1, :] == slot, 1.0, hit)
            matrix[g] = hit.astype(matrix.dtype)

    parts = unwoven(tokens_ref[...], groups, per_token)
    found = [dot(matrix[g], parts[g]) for g in range(groups)]
    out_ref[...] = woven(found, per_row).astype(out_ref.dtype)


def pick(rows_t, tokens, width, per_token, per_row, tile):
    groups, top, count = rows_t.shape
    total = N_XC * per_row
    return pl.pallas_call(
        functools.partial(pick_kernel, groups, per_token, per_row),
        grid=(width // tile,),
        in_specs=[
            pl.BlockSpec((groups, top, count), lambda j: (0, 0, 0)),
            pl.BlockSpec((groups * count, tile), lambda j: (0, j)),
        ],
        out_specs=pl.BlockSpec((groups * total, tile), lambda j: (0, j)),
        out_shape=jax.ShapeDtypeStruct((groups * total, width), jnp.bfloat16),
        scratch_shapes=[pltpu.VMEM((groups, total, count), jnp.bfloat16)],
        compiler_params=pltpu.CompilerParams(vmem_limit_bytes=VMEM),
        cost_estimate=pl.CostEstimate(
            flops=2 * groups * total * count * width, bytes_accessed=2 * groups * (total + count) * width, transcendentals=0
        ),
    )(rows_t, tokens)


def mix_kernel(groups, per_token, per_row, rows_ref, gates_ref, back_ref, out_ref, matrix):
    @pl.when(pl.program_id(0) == 0)
    def _():
        for g in range(groups):
            slot = lax.broadcasted_iota(jnp.int32, matrix.shape[1:], 1)
            total = jnp.zeros(matrix.shape[1:], jnp.float32)
            for k in range(rows_ref.shape[2]):
                total = jnp.where(rows_ref[g, :, k : k + 1] == slot, gates_ref[g, :, k : k + 1], total)
            matrix[g] = total.astype(matrix.dtype)

    back = back_ref[...]
    if groups > 1:
        parts = [p.astype(jnp.bfloat16) for p in unwoven(back.astype(jnp.float32), groups, per_row)]
    else:
        parts = [back]
    found = [dot(matrix[g], parts[g]) for g in range(groups)]
    out_ref[...] = woven(found, per_token).astype(out_ref.dtype)


def mix(rows, gates, back, per_token, per_row, tile):
    groups, count, top = rows.shape
    total = N_XC * per_row
    width = back.shape[1]
    return pl.pallas_call(
        functools.partial(mix_kernel, groups, per_token, per_row),
        grid=(width // tile,),
        in_specs=[
            pl.BlockSpec((groups, count, top), lambda j: (0, 0, 0)),
            pl.BlockSpec((groups, count, top), lambda j: (0, 0, 0)),
            pl.BlockSpec((groups * total, tile), lambda j: (0, j)),
        ],
        out_specs=pl.BlockSpec((groups * count, tile), lambda j: (0, j)),
        out_shape=jax.ShapeDtypeStruct((groups * count, width), jnp.bfloat16),
        scratch_shapes=[pltpu.VMEM((groups, count, total), jnp.bfloat16)],
        compiler_params=pltpu.CompilerParams(vmem_limit_bytes=VMEM),
        cost_estimate=pl.CostEstimate(
            flops=2 * groups * total * count * width, bytes_accessed=2 * groups * (total + count) * width, transcendentals=0
        ),
    )(rows, gates, back)


def down_kernel(has_add, hidden_ref, own_ref, low_ref, high_ref, *refs):
    weights = jnp.concatenate([own_ref[...], low_ref[...], high_ref[...]], axis=0)
    result = dot(hidden_ref[...], weights)
    if has_add:
        result = result + refs[0][...].astype(jnp.float32)
    refs[-1][...] = result.astype(refs[-1].dtype)


def down(hidden, own, low, high, first, width, tile, add=None):
    count, units = hidden.shape
    at = first // tile
    half = low.shape[0]
    extra = [] if add is None else [add]
    return pl.pallas_call(
        functools.partial(down_kernel, add is not None),
        grid=(width // tile,),
        in_specs=[
            pl.BlockSpec((count, units), lambda j: (0, 0)),
            pl.BlockSpec((own.shape[0], tile), lambda j: (0, j + at)),
            pl.BlockSpec((half, tile), lambda j: (0, j + at)),
            pl.BlockSpec((half, tile), lambda j: (0, j + at)),
        ]
        + [pl.BlockSpec((count, tile), lambda j: (0, j))] * len(extra),
        out_specs=pl.BlockSpec((count, tile), lambda j: (0, j)),
        out_shape=jax.ShapeDtypeStruct((count, width), jnp.bfloat16),
        compiler_params=pltpu.CompilerParams(vmem_limit_bytes=VMEM),
        cost_estimate=pl.CostEstimate(
            flops=2 * count * units * width, bytes_accessed=2 * (units + 2 * count) * width, transcendentals=0
        ),
    )(hidden, own, low, high, *extra)


def dot(a, b):
    return jnp.dot(a, b, preferred_element_type=jnp.float32)


def exchange(rows):
    parts = rows.reshape(N_XC, rows.shape[0] // N_XC, rows.shape[1])
    return lax.all_to_all(parts, XC, split_axis=0, concat_axis=0, tiled=True)


def local(tokens, expert_ids, gate_values, swap_mask, gate_weight, up_weight, down_weight):
    tok_count, width = tokens.shape
    top = expert_ids.shape[1]
    experts = N_Z * N_XC
    capacity = min(tok_count, tok_count * top // experts + 1)
    cut = width // 2
    tile = min(512, cut)
    w_gate, w_up, w_down = gate_weight[0], up_weight[0], down_weight[0]
    units = w_gate.shape[1]
    half = units // 2

    held_by, rank = codes_of(expert_ids, swap_mask, capacity)
    extra = jnp.concatenate(
        [held_by.astype(jnp.bfloat16), rank.astype(jnp.bfloat16), gate_values.astype(jnp.bfloat16)], axis=1
    )
    extra = jnp.pad(extra, ((0, 0), (0, EXTRA - extra.shape[1])))
    late_in = jnp.concatenate([tokens[:, cut:], extra], axis=1)
    early_in = jnp.concatenate([tokens[:, :cut], extra], axis=1)
    early_other = shift(early_in, Y, 2)

    low = jnp.concatenate([w_gate[:, :half], w_up[:, :half]], axis=1)
    high = jnp.concatenate([w_gate[:, half:], w_up[:, half:]], axis=1)
    low, high = after((low, high), early_in)
    low_in, high_in = shift(low, Y, -1), shift(high, Y, 1)
    down_parts = after((w_down[:half], w_down[half:]), low_in, high_in)
    down_low, down_high = shift(down_parts[0], Y, -1), shift(down_parts[1], Y, 1)

    late_all = lax.all_gather(late_in, Z, axis=0, tiled=True)
    early_pair = jnp.concatenate([early_in, early_other], axis=0)
    early_pair = after(early_pair, late_in)
    early_all = lax.all_gather(early_pair, Z, axis=0, tiled=True)

    per = N_Z * capacity
    total = N_XC * 2 * per
    late_width = width - cut
    late_pairs, late_gates = pairs_of(late_all[:, late_width:], top, capacity)
    late_rows = pick(late_pairs.T[None], late_all, late_width, tok_count, per, tile)
    late_own = exchange(late_rows)
    part = N_XC // 2
    late_other_0 = shift(late_own[:part], Y, 2)
    late_other_1 = shift(after(late_own[part:], late_other_0), Y, 2)
    late_other = jnp.concatenate([late_other_0, late_other_1], axis=0)

    by_group = early_all[:, cut:].reshape(N_Z, 2, tok_count, EXTRA)
    early_pairs, early_gates = zip(
        *(pairs_of(by_group[:, g].reshape(N_Z * tok_count, EXTRA), top, capacity) for g in range(2))
    )
    early_pairs, early_gates = jnp.stack(early_pairs), jnp.stack(early_gates)
    early_rows = pick(jnp.swapaxes(early_pairs, 1, 2), early_all, cut, tok_count, per, tile)
    early_rows = after(early_rows, late_own, late_other_0, low_in, high_in)
    early_got = exchange(early_rows).reshape(total, cut)
    late_got = jnp.stack([late_own, late_other], axis=1).reshape(total, late_width)

    w_own = jnp.concatenate([w_gate, w_up], axis=1)
    w_in = jnp.concatenate([low_in, high_in], axis=1)
    act_own = dot(late_got, w_own[cut:]) + dot(early_got, w_own[:cut])
    act_in = dot(late_got, w_in[cut:]) + dot(early_got, w_in[:cut])
    hidden = jnp.concatenate(
        [
            jax.nn.silu(act_own[:, :units]) * act_own[:, units:],
            jax.nn.silu(act_in[:, :half]) * act_in[:, half:units],
            jax.nn.silu(act_in[:, units : units + half]) * act_in[:, units + half :],
        ],
        axis=1,
    ).astype(jnp.bfloat16)
    by_group = hidden.reshape(N_XC, 2, per, 2 * units)
    hidden_own = by_group[:, 0].reshape(N_XC * per, 2 * units)
    hidden_other = by_group[:, 1].reshape(N_XC * per, 2 * units)
    late_for_other = down(hidden_other, w_down, down_low, down_high, cut, late_width, tile)
    late_from_other = shift(late_for_other, Y, 2)
    early_out = down(after(hidden, late_for_other), w_down, down_low, down_high, 0, cut, tile)
    early_back = after(exchange(early_out), late_from_other).reshape(total, cut)
    early_mixed = mix(early_pairs, early_gates, early_back, tok_count, per, tile)
    early_sum = lax.psum_scatter(early_mixed, Z, scatter_dimension=0, tiled=True)
    early_final = early_sum[:tok_count].astype(jnp.float32) + shift(early_sum[tok_count:], Y, 2).astype(jnp.float32)

    late_out = down(hidden_own, w_down, down_low, down_high, cut, late_width, tile, late_from_other)
    late_back = exchange(late_out).reshape(N_XC * per, late_width)
    late_mixed = mix(late_pairs[None], late_gates[None], late_back, tok_count, per, tile)
    late_final = lax.psum_scatter(late_mixed, Z, scatter_dimension=0, tiled=True)
    return jnp.concatenate([early_final.astype(jnp.bfloat16), late_final], axis=1)


def solution(mesh):
    fine = Mesh(mesh.devices.reshape(N_Y, N_Z, N_XC // 2, 2), ALL)
    experts = (Z, X, C)
    placed = (
        P(ALL, None),
        P(ALL, None),
        P(ALL, None),
        P(),
        P(experts, None, Y),
        P(experts, None, Y),
        P(experts, Y, None),
    )
    return jax.shard_map(local, mesh=fine, in_specs=placed, out_specs=P(ALL, None), check_vma=False)
```

```python
import functools
import jax
import jax.numpy as jnp
from jax import lax
from jax.experimental import pallas as pl
from jax.experimental.pallas import tpu as pltpu
from jax.sharding import Mesh, PartitionSpec as P

Y, Z, X, C = "y", "z", "x", "c"
ALL = (Y, Z, X, C)
XC = (X, C)
N_Y, N_Z, N_XC = 4, 8, 8
EXTRA = 128
VMEM = 20 << 20
FREE = pl.CostEstimate(flops=0, bytes_accessed=0, transcendentals=0)


def shift(block, axis, by):
    count = lax.axis_size(axis)
    return lax.ppermute(block, axis, [(i, (i + by) % count) for i in range(count)])


def after(value, *others):
    return lax.optimization_barrier((value, *others))[0]


def codes_kernel(mask_ref, tokens_ref, own_ref, other_ref, out_ref):
    count, width = tokens_ref.shape
    top = own_ref.shape[0] // 2
    experts = N_Z * N_XC
    slot = lax.broadcasted_iota(jnp.int32, (count, experts), 1)
    own = lax.broadcasted_iota(jnp.int32, (1, experts), 1)
    mask = jnp.concatenate([mask_ref[...], mask_ref[...]], axis=1)
    holder = jnp.where(mask == 1, own ^ (experts // 2), own).astype(jnp.float32)
    row = lax.broadcasted_iota(jnp.int32, (count, count), 0)
    earlier = (lax.broadcasted_iota(jnp.int32, (count, count), 1) < row).astype(jnp.bfloat16)
    lane = lax.broadcasted_iota(jnp.int32, (count, EXTRA), 1)
    out = jnp.zeros((count, EXTRA), jnp.float32)
    for ref, first in ((own_ref, 0), (other_ref, EXTRA // 2)):
        pairs = ref[...].T
        ids = pairs[:, :top].astype(jnp.int32)
        hits = [(ids[:, k : k + 1] == slot).astype(jnp.float32) for k in range(top)]
        chosen = functools.reduce(lambda p, q: p + q, hits)
        before = dot(earlier, chosen.astype(jnp.bfloat16))
        for k in range(top):
            out = jnp.where(lane == first + k, jnp.sum(hits[k] * holder, axis=1, keepdims=True), out)
            out = jnp.where(lane == first + top + k, jnp.sum(hits[k] * before, axis=1, keepdims=True), out)
            out = jnp.where(lane == first + 2 * top + k, pairs[:, top + k : top + k + 1], out)
    out_ref[:, :width] = tokens_ref[...]
    out_ref[:, width:] = out.astype(out_ref.dtype)


def with_codes(mask, tokens, own, other):
    return pl.pallas_call(
        codes_kernel,
        out_shape=jax.ShapeDtypeStruct((tokens.shape[0], tokens.shape[1] + EXTRA), jnp.bfloat16),
        cost_estimate=FREE,
    )(mask[None], tokens, own, other)


def rows_of(held_by, rank, token, per_z, capacity, z):
    held_by = held_by.astype(jnp.int32)
    row = ((held_by & (N_XC - 1)) * N_Z + token // per_z) * capacity + rank.astype(jnp.int32)
    return jnp.where(held_by // N_XC == z, row, -1)


def picks_kernel(first, top, capacity, z_ref, extra_ref, out_ref):
    across = extra_ref[...].astype(jnp.float32).T[first : first + 2 * top]
    count = across.shape[1]
    token = lax.broadcasted_iota(jnp.int32, (top, count), 1)
    row = rows_of(across[:top], across[top:], token, count // N_Z, capacity, z_ref[0])
    slot = lax.broadcasted_iota(jnp.int32, out_ref.shape, 0)
    hit = jnp.zeros(out_ref.shape, jnp.float32)
    for k in range(top):
        hit = jnp.where(row[k : k + 1] == slot, 1.0, hit)
    out_ref[...] = hit.astype(out_ref.dtype)


def mixes_kernel(first, top, capacity, z_ref, extra_ref, out_ref):
    values = extra_ref[:, first : first + 3 * top].astype(jnp.float32)
    count = values.shape[0]
    token = lax.broadcasted_iota(jnp.int32, (count, top), 0)
    row = rows_of(values[:, :top], values[:, top : 2 * top], token, count // N_Z, capacity, z_ref[0])
    slot = lax.broadcasted_iota(jnp.int32, out_ref.shape, 1)
    total = jnp.zeros(out_ref.shape, jnp.float32)
    for k in range(top):
        total = jnp.where(row[:, k : k + 1] == slot, values[:, 2 * top + k : 2 * top + k + 1], total)
    out_ref[...] = total.astype(out_ref.dtype)


def matrix(kernel, gathered, first, top, capacity, shape):
    count, width = gathered.shape
    return pl.pallas_call(
        functools.partial(kernel, first, top, capacity),
        grid=(1,),
        in_specs=[
            pl.BlockSpec(memory_space=pltpu.SMEM),
            pl.BlockSpec((count, EXTRA), lambda j: (0, width // EXTRA - 1)),
        ],
        out_specs=pl.BlockSpec(shape, lambda j: (0, 0)),
        out_shape=jax.ShapeDtypeStruct(shape, jnp.bfloat16),
        compiler_params=pltpu.CompilerParams(vmem_limit_bytes=VMEM),
        cost_estimate=FREE,
    )(lax.axis_index(Z).astype(jnp.int32)[None], gathered)


def apply_kernel(matrix_ref, value_ref, out_ref):
    out_ref[...] = dot(matrix_ref[...], value_ref[...]).astype(out_ref.dtype)


def apply(matrix, value, first, width, tile):
    rows, inner = matrix.shape
    at = first // tile
    return pl.pallas_call(
        apply_kernel,
        grid=(width // tile,),
        in_specs=[pl.BlockSpec((rows, inner), lambda j: (0, 0)), pl.BlockSpec((inner, tile), lambda j: (0, j + at))],
        out_specs=pl.BlockSpec((rows, tile), lambda j: (0, j)),
        out_shape=jax.ShapeDtypeStruct((rows, width), jnp.bfloat16),
        compiler_params=pltpu.CompilerParams(vmem_limit_bytes=VMEM),
        cost_estimate=FREE,
    )(matrix, value)


def sides_kernel(bounds, gate_ref, up_ref, *out_refs):
    half = gate_ref.shape[1] // 2
    gate, up = gate_ref[...], up_ref[...]
    low = jnp.concatenate([gate[:, :half], up[:, :half]], axis=1)
    high = jnp.concatenate([gate[:, half:], up[:, half:]], axis=1)
    step = pl.program_id(0)
    for i, (first, last) in enumerate(zip(bounds, bounds[1:])):

        @pl.when((step >= first) & (step < last))
        def _():
            out_refs[2 * i][...] = low
            out_refs[2 * i + 1][...] = high


def sides(gate, up, bounds, tile):
    rows, units = gate.shape
    steps = [bound // tile for bound in bounds]

    def spec(first, last):
        return pl.BlockSpec((tile, units), lambda j: (jnp.clip(j - first, 0, last - first - 1), 0))

    ranges = [r for r in zip(bounds, bounds[1:]) for _ in range(2)]
    outs = pl.pallas_call(
        functools.partial(sides_kernel, steps),
        grid=(rows // tile,),
        in_specs=[pl.BlockSpec((tile, units), lambda j: (j, 0))] * 2,
        out_specs=[spec(first // tile, last // tile) for first, last in ranges],
        out_shape=[jax.ShapeDtypeStruct((last - first, units), gate.dtype) for first, last in ranges],
        compiler_params=pltpu.CompilerParams(vmem_limit_bytes=VMEM),
        cost_estimate=FREE,
    )(gate, up)
    return list(zip(outs[::2], outs[1::2]))


def down_kernel(has_add, hidden_ref, own_ref, low_ref, high_ref, *refs):
    weights = jnp.concatenate([own_ref[...], low_ref[...], high_ref[...]], axis=0)
    result = dot(hidden_ref[...], weights)
    if has_add:
        result = result + refs[0][...].astype(jnp.float32)
    refs[-1][...] = result.astype(refs[-1].dtype)


def down(hidden, own, low, high, first, width, tile, add=None):
    count, units = hidden.shape
    at = first // tile
    half = low.shape[0]
    extra = [] if add is None else [add]
    return pl.pallas_call(
        functools.partial(down_kernel, add is not None),
        grid=(width // tile,),
        in_specs=[
            pl.BlockSpec((count, units), lambda j: (0, 0)),
            pl.BlockSpec((own.shape[0], tile), lambda j: (0, j + at)),
            pl.BlockSpec((half, tile), lambda j: (0, j + at)),
            pl.BlockSpec((half, tile), lambda j: (0, j + at)),
        ]
        + [pl.BlockSpec((count, tile), lambda j: (0, j))] * len(extra),
        out_specs=pl.BlockSpec((count, tile), lambda j: (0, j)),
        out_shape=jax.ShapeDtypeStruct((count, width), jnp.bfloat16),
        compiler_params=pltpu.CompilerParams(vmem_limit_bytes=VMEM),
        cost_estimate=FREE,
    )(hidden, own, low, high, *extra)


def dot(a, b):
    return jnp.dot(a, b, preferred_element_type=jnp.float32)


def exchange(rows):
    parts = rows.reshape(N_XC, rows.shape[0] // N_XC, rows.shape[1])
    return lax.all_to_all(parts, XC, split_axis=0, concat_axis=0, tiled=True).reshape(rows.shape)


def local(tokens, expert_ids, gate_values, swap_mask, gate_weight, up_weight, down_weight):
    tok_count, width = tokens.shape
    top = expert_ids.shape[1]
    experts = N_Z * N_XC
    capacity = min(tok_count, tok_count * top // experts + 1)
    cut = width // 2
    tile = min(512, cut)
    w_gate, w_up, w_down = gate_weight[0], up_weight[0], down_weight[0]
    units = w_gate.shape[1]
    half = units // 2

    pairs = jnp.concatenate([expert_ids.T.astype(jnp.float32), gate_values.T], axis=0)
    own_tokens = with_codes(swap_mask, tokens, pairs, shift(pairs, Y, 2))
    other_tokens = shift(after(tokens[:, :cut], own_tokens), Y, 2)

    def swap(parts):
        return shift(parts[0], Y, -1), shift(parts[1], Y, 1)

    bounds = [0, width // 16 * 6, width // 16 * 11, width]
    side_2, side_1, side_0 = sides(after(w_gate, own_tokens), w_up, bounds, width // 16)
    down_low, down_high = swap(after((w_down[:half], w_down[half:]), pairs))
    side_0 = swap(after(side_0, down_low, down_high, other_tokens))
    side_1 = swap(after(side_1, *side_0))
    side_2 = swap(after(side_2, *side_1))

    own_all = lax.all_gather(own_tokens, Z, axis=0, tiled=True)
    other_all = lax.all_gather(after(other_tokens, own_tokens), Z, axis=0, tiled=True)
    own_all = after(own_all, down_low, down_high)

    late_width = width - cut
    rows, count = N_XC * N_Z * capacity, N_Z * tok_count
    second = EXTRA // 2
    pick_own = matrix(picks_kernel, own_all, 0, top, capacity, (rows, count))
    late_rows = apply(pick_own, own_all, cut, late_width, tile)
    own_rows = apply(after(pick_own, late_rows), own_all, 0, cut, tile)
    own_late = exchange(after(late_rows, own_rows, *side_0))
    own_early = exchange(after(own_rows, own_late, *side_1))
    mix_own = matrix(mixes_kernel, after(own_all, own_rows), 0, top, capacity, (count, rows))
    pick_other = matrix(picks_kernel, after(own_all, mix_own), second, top, capacity, (rows, count))
    other_rows = apply(pick_other, other_all, 0, cut, tile)
    other_early = exchange(after(other_rows, own_early, *side_2))
    mix_other = matrix(mixes_kernel, after(own_all, other_rows), second, top, capacity, (count, rows))
    other_late = shift(after(own_late, *side_2), Y, 2)

    w_own = jnp.concatenate([w_gate, w_up], axis=1)
    w_in = jnp.concatenate([jnp.concatenate(side, axis=1) for side in (side_2, side_1, side_0)], axis=0)

    def hidden_of(late, early):
        act_own = dot(late, w_own[cut:]) + dot(early, w_own[:cut])
        act_in = dot(late, w_in[cut:]) + dot(early, w_in[:cut])
        return jnp.concatenate(
            [
                jax.nn.silu(act_own[:, :units]) * act_own[:, units:],
                jax.nn.silu(act_in[:, :half]) * act_in[:, half:units],
                jax.nn.silu(act_in[:, units : units + half]) * act_in[:, units + half :],
            ],
            axis=1,
        ).astype(jnp.bfloat16)

    early_down = (w_down, down_low, down_high, 0, cut, tile)
    late_down = (w_down, down_low, down_high, cut, late_width, tile)
    hidden_own = hidden_of(own_late, own_early)
    own_out = down(hidden_own, *early_down)
    own_back = exchange(after(own_out, other_early))
    hidden_other = hidden_of(other_late, other_early)
    late_for_other = down(hidden_other, *late_down)
    late_from_other = shift(late_for_other, Y, 2)
    other_out = down(after(hidden_other, late_for_other), *early_down)

    own_mixed = apply(mix_own, after(own_back, other_out), 0, cut, tile)
    own_sum = lax.psum_scatter(own_mixed, Z, scatter_dimension=0, tiled=True)
    other_back = after(exchange(other_out), own_sum)
    other_mixed = apply(mix_other, other_back, 0, cut, tile)
    other_sum = lax.psum_scatter(after(other_mixed, late_from_other), Z, scatter_dimension=0, tiled=True)
    early_final = own_sum.astype(jnp.float32) + shift(other_sum, Y, 2).astype(jnp.float32)

    late_out = down(hidden_own, *late_down, late_from_other)
    late_back = exchange(after(late_out, other_mixed))
    late_final = lax.psum_scatter(apply(mix_own, late_back, 0, late_width, tile), Z, scatter_dimension=0, tiled=True)
    return jnp.concatenate([early_final.astype(jnp.bfloat16), late_final], axis=1)


def solution(mesh):
    fine = Mesh(mesh.devices.reshape(N_Y, N_Z, N_XC // 2, 2), ALL)
    experts = (Z, X, C)
    placed = (
        P(ALL, None),
        P(ALL, None),
        P(ALL, None),
        P(),
        P(experts, None, Y),
        P(experts, None, Y),
        P(experts, Y, None),
    )
    return jax.shard_map(local, mesh=fine, in_specs=placed, out_specs=P(ALL, None), check_vma=False)
```

```python
import functools
import jax
import jax.numpy as jnp
from jax import lax
from jax.experimental import pallas as pl
from jax.experimental.pallas import tpu as pltpu
from jax.sharding import Mesh, PartitionSpec as P

Y, Z, X, C = "y", "z", "x", "c"
ALL = (Y, Z, X, C)
XC = (X, C)
N_Y, N_Z, N_XC = 4, 8, 8
EXTRA = 128
VMEM = 20 << 20
FREE = pl.CostEstimate(flops=0, bytes_accessed=0, transcendentals=0)


def shift(block, axis, by):
    count = lax.axis_size(axis)
    return lax.ppermute(block, axis, [(i, (i + by) % count) for i in range(count)])


def after(value, *others):
    return lax.optimization_barrier((value, *others))[0]


def codes_kernel(mask_ref, tokens_ref, own_ref, other_ref, out_ref):
    count, width = tokens_ref.shape
    top = own_ref.shape[0] // 2
    experts = N_Z * N_XC
    slot = lax.broadcasted_iota(jnp.int32, (count, experts), 1)
    own = lax.broadcasted_iota(jnp.int32, (1, experts), 1)
    mask = jnp.concatenate([mask_ref[...], mask_ref[...]], axis=1)
    holder = jnp.where(mask == 1, own ^ (experts // 2), own).astype(jnp.float32)
    row = lax.broadcasted_iota(jnp.int32, (count, count), 0)
    earlier = (lax.broadcasted_iota(jnp.int32, (count, count), 1) < row).astype(jnp.bfloat16)
    lane = lax.broadcasted_iota(jnp.int32, (count, EXTRA), 1)
    out = jnp.zeros((count, EXTRA), jnp.float32)
    for ref, first in ((own_ref, 0), (other_ref, EXTRA // 2)):
        pairs = ref[...].T
        ids = pairs[:, :top].astype(jnp.int32)
        hits = [(ids[:, k : k + 1] == slot).astype(jnp.float32) for k in range(top)]
        chosen = functools.reduce(lambda p, q: p + q, hits)
        before = dot(earlier, chosen.astype(jnp.bfloat16))
        for k in range(top):
            out = jnp.where(lane == first + k, jnp.sum(hits[k] * holder, axis=1, keepdims=True), out)
            out = jnp.where(lane == first + top + k, jnp.sum(hits[k] * before, axis=1, keepdims=True), out)
            out = jnp.where(lane == first + 2 * top + k, pairs[:, top + k : top + k + 1], out)
    out_ref[:, :width] = tokens_ref[...]
    out_ref[:, width:] = out.astype(out_ref.dtype)


def with_codes(mask, tokens, own, other):
    return pl.pallas_call(
        codes_kernel,
        out_shape=jax.ShapeDtypeStruct((tokens.shape[0], tokens.shape[1] + EXTRA), jnp.bfloat16),
        cost_estimate=FREE,
    )(mask[None], tokens, own, other)


def rows_of(held_by, rank, token, per_z, capacity, z):
    held_by = held_by.astype(jnp.int32)
    row = ((held_by & (N_XC - 1)) * N_Z + token // per_z) * capacity + rank.astype(jnp.int32)
    return jnp.where(held_by // N_XC == z, row, -1)


def picks_kernel(first, top, capacity, z_ref, extra_ref, out_ref):
    across = extra_ref[...].astype(jnp.float32).T[first : first + 2 * top]
    count = across.shape[1]
    token = lax.broadcasted_iota(jnp.int32, (top, count), 1)
    row = rows_of(across[:top], across[top:], token, count // N_Z, capacity, z_ref[0])
    slot = lax.broadcasted_iota(jnp.int32, out_ref.shape, 0)
    hit = jnp.zeros(out_ref.shape, jnp.float32)
    for k in range(top):
        hit = jnp.where(row[k : k + 1] == slot, 1.0, hit)
    out_ref[...] = hit.astype(out_ref.dtype)


def mixes_kernel(first, top, capacity, z_ref, extra_ref, out_ref):
    values = extra_ref[:, first : first + 3 * top].astype(jnp.float32)
    count = values.shape[0]
    token = lax.broadcasted_iota(jnp.int32, (count, top), 0)
    row = rows_of(values[:, :top], values[:, top : 2 * top], token, count // N_Z, capacity, z_ref[0])
    slot = lax.broadcasted_iota(jnp.int32, out_ref.shape, 1)
    total = jnp.zeros(out_ref.shape, jnp.float32)
    for k in range(top):
        total = jnp.where(row[:, k : k + 1] == slot, values[:, 2 * top + k : 2 * top + k + 1], total)
    out_ref[...] = total.astype(out_ref.dtype)


def matrix(kernel, gathered, first, top, capacity, shape):
    count, width = gathered.shape
    return pl.pallas_call(
        functools.partial(kernel, first, top, capacity),
        grid=(1,),
        in_specs=[
            pl.BlockSpec(memory_space=pltpu.SMEM),
            pl.BlockSpec((count, EXTRA), lambda j: (0, width // EXTRA - 1)),
        ],
        out_specs=pl.BlockSpec(shape, lambda j: (0, 0)),
        out_shape=jax.ShapeDtypeStruct(shape, jnp.bfloat16),
        compiler_params=pltpu.CompilerParams(vmem_limit_bytes=VMEM),
        cost_estimate=FREE,
    )(lax.axis_index(Z).astype(jnp.int32)[None], gathered)


def apply_kernel(matrix_ref, value_ref, out_ref):
    out_ref[...] = dot(matrix_ref[...], value_ref[...]).astype(out_ref.dtype)


def apply(matrix, value, first, width, tile):
    rows, inner = matrix.shape
    at = first // tile
    return pl.pallas_call(
        apply_kernel,
        grid=(width // tile,),
        in_specs=[pl.BlockSpec((rows, inner), lambda j: (0, 0)), pl.BlockSpec((inner, tile), lambda j: (0, j + at))],
        out_specs=pl.BlockSpec((rows, tile), lambda j: (0, j)),
        out_shape=jax.ShapeDtypeStruct((rows, width), jnp.bfloat16),
        compiler_params=pltpu.CompilerParams(vmem_limit_bytes=VMEM),
        cost_estimate=FREE,
    )(matrix, value)


def sides_kernel(bounds, gate_ref, up_ref, *out_refs):
    half = gate_ref.shape[1] // 2
    gate, up = gate_ref[...], up_ref[...]
    low = jnp.concatenate([gate[:, :half], up[:, :half]], axis=1)
    high = jnp.concatenate([gate[:, half:], up[:, half:]], axis=1)
    step = pl.program_id(0)
    for i, (first, last) in enumerate(zip(bounds, bounds[1:])):

        @pl.when((step >= first) & (step < last))
        def _():
            out_refs[2 * i][...] = low
            out_refs[2 * i + 1][...] = high


def sides(gate, up, bounds, tile):
    rows, units = gate.shape
    steps = [bound // tile for bound in bounds]

    def spec(first, last):
        return pl.BlockSpec((tile, units), lambda j: (jnp.clip(j - first, 0, last - first - 1), 0))

    ranges = [r for r in zip(bounds, bounds[1:]) for _ in range(2)]
    outs = pl.pallas_call(
        functools.partial(sides_kernel, steps),
        grid=(rows // tile,),
        in_specs=[pl.BlockSpec((tile, units), lambda j: (j, 0))] * 2,
        out_specs=[spec(first // tile, last // tile) for first, last in ranges],
        out_shape=[jax.ShapeDtypeStruct((last - first, units), gate.dtype) for first, last in ranges],
        compiler_params=pltpu.CompilerParams(vmem_limit_bytes=VMEM),
        cost_estimate=FREE,
    )(gate, up)
    return list(zip(outs[::2], outs[1::2]))


def down_kernel(has_add, hidden_ref, own_ref, low_ref, high_ref, *refs):
    weights = jnp.concatenate([own_ref[...], low_ref[...], high_ref[...]], axis=0)
    result = dot(hidden_ref[...], weights)
    if has_add:
        result = result + refs[0][...].astype(jnp.float32)
    refs[-1][...] = result.astype(refs[-1].dtype)


def down(hidden, own, low, high, first, width, tile, add=None):
    count, units = hidden.shape
    at = first // tile
    half = low.shape[0]
    extra = [] if add is None else [add]
    return pl.pallas_call(
        functools.partial(down_kernel, add is not None),
        grid=(width // tile,),
        in_specs=[
            pl.BlockSpec((count, units), lambda j: (0, 0)),
            pl.BlockSpec((own.shape[0], tile), lambda j: (0, j + at)),
            pl.BlockSpec((half, tile), lambda j: (0, j + at)),
            pl.BlockSpec((half, tile), lambda j: (0, j + at)),
        ]
        + [pl.BlockSpec((count, tile), lambda j: (0, j))] * len(extra),
        out_specs=pl.BlockSpec((count, tile), lambda j: (0, j)),
        out_shape=jax.ShapeDtypeStruct((count, width), jnp.bfloat16),
        compiler_params=pltpu.CompilerParams(vmem_limit_bytes=VMEM),
        cost_estimate=FREE,
    )(hidden, own, low, high, *extra)


def dot(a, b):
    return jnp.dot(a, b, preferred_element_type=jnp.float32)


def exchange(rows):
    parts = rows.reshape(N_XC, rows.shape[0] // N_XC, rows.shape[1])
    return lax.all_to_all(parts, XC, split_axis=0, concat_axis=0, tiled=True).reshape(rows.shape)


def local(tokens, expert_ids, gate_values, swap_mask, gate_weight, up_weight, down_weight):
    tok_count, width = tokens.shape
    top = expert_ids.shape[1]
    experts = N_Z * N_XC
    capacity = min(tok_count, tok_count * top // experts + 1)
    cut = width // 2
    tile = min(512, cut)
    back = width // 8 * 5
    rest = width - back
    w_gate, w_up, w_down = gate_weight[0], up_weight[0], down_weight[0]
    units = w_gate.shape[1]
    half = units // 2

    pairs = jnp.concatenate([expert_ids.T.astype(jnp.float32), gate_values.T], axis=0)
    down_parts = after((w_down[:half], w_down[half:]), pairs)
    pairs_other, *down_parts = lax.optimization_barrier((shift(pairs, Y, 2), *down_parts))
    own_tokens = with_codes(swap_mask, tokens, pairs, pairs_other)
    other_tokens = shift(after(tokens[:, :cut], own_tokens), Y, 2)

    def swap(parts):
        return shift(parts[0], Y, -1), shift(parts[1], Y, 1)

    bounds = [0, width // 16 * 6, width // 16 * 11, width]
    side_2, side_1, side_0 = sides(after(w_gate, own_tokens), w_up, bounds, width // 16)
    down_low, down_high = swap(down_parts)
    side_0 = swap(after(side_0, down_low, down_high, other_tokens))
    side_1 = swap(after(side_1, *side_0))
    side_2 = swap(after(side_2, *side_1))

    own_all = lax.all_gather(own_tokens, Z, axis=0, tiled=True)
    other_all = lax.all_gather(after(other_tokens, own_tokens), Z, axis=0, tiled=True)
    own_all = after(own_all, down_low, down_high)

    late_width = width - cut
    rows, count = N_XC * N_Z * capacity, N_Z * tok_count
    second = EXTRA // 2
    pick_own = matrix(picks_kernel, own_all, 0, top, capacity, (rows, count))
    late_rows = apply(pick_own, own_all, cut, late_width, tile)
    own_rows = apply(after(pick_own, late_rows), own_all, 0, cut, tile)
    own_late = exchange(after(late_rows, own_rows, *side_0))
    own_early = exchange(after(own_rows, own_late, *side_1))
    mix_own = matrix(mixes_kernel, after(own_all, own_rows), 0, top, capacity, (count, rows))
    pick_other = matrix(picks_kernel, after(own_all, mix_own), second, top, capacity, (rows, count))
    other_rows = apply(pick_other, other_all, 0, cut, tile)
    other_early = exchange(after(other_rows, own_early, *side_2))
    mix_other = matrix(mixes_kernel, after(own_all, other_rows), second, top, capacity, (count, rows))
    other_late = shift(after(own_late, *side_2), Y, 2)

    w_own = jnp.concatenate([w_gate, w_up], axis=1)
    w_in = jnp.concatenate([jnp.concatenate(side, axis=1) for side in (side_2, side_1, side_0)], axis=0)

    def hidden_of(late, early):
        act_own = dot(late, w_own[cut:]) + dot(early, w_own[:cut])
        act_in = dot(late, w_in[cut:]) + dot(early, w_in[:cut])
        return jnp.concatenate(
            [
                jax.nn.silu(act_own[:, :units]) * act_own[:, units:],
                jax.nn.silu(act_in[:, :half]) * act_in[:, half:units],
                jax.nn.silu(act_in[:, units : units + half]) * act_in[:, units + half :],
            ],
            axis=1,
        ).astype(jnp.bfloat16)

    early_down = (w_down, down_low, down_high, 0, back, tile)
    late_down = (w_down, down_low, down_high, back, rest, tile)
    hidden_own = hidden_of(own_late, own_early)
    own_out = down(hidden_own, *early_down)
    own_back = exchange(after(own_out, other_early))
    hidden_other = hidden_of(other_late, other_early)
    late_for_other = down(hidden_other, *late_down)
    late_from_other = shift(late_for_other, Y, 2)
    other_out = down(after(hidden_other, late_for_other), *early_down)

    own_mixed = apply(mix_own, after(own_back, other_out), 0, back, tile)
    own_sum = lax.psum_scatter(own_mixed, Z, scatter_dimension=0, tiled=True)
    other_back = exchange(other_out)
    other_mixed = apply(mix_other, other_back, 0, back, tile)
    other_sum = lax.psum_scatter(after(other_mixed, late_from_other, own_sum), Z, scatter_dimension=0, tiled=True)
    early_final = own_sum.astype(jnp.float32) + shift(other_sum, Y, 2).astype(jnp.float32)

    late_out = down(hidden_own, *late_down, late_from_other)
    late_back = exchange(after(late_out, other_mixed))
    late_final = lax.psum_scatter(apply(mix_own, late_back, 0, rest, tile), Z, scatter_dimension=0, tiled=True)
    result = jnp.pad(early_final.astype(jnp.bfloat16), ((0, 0), (0, rest)))
    return lax.dynamic_update_slice(result, late_final, (0, back))


def solution(mesh):
    fine = Mesh(mesh.devices.reshape(N_Y, N_Z, N_XC // 2, 2), ALL)
    experts = (Z, X, C)
    placed = (
        P(ALL, None),
        P(ALL, None),
        P(ALL, None),
        P(),
        P(experts, None, Y),
        P(experts, None, Y),
        P(experts, Y, None),
    )
    return jax.shard_map(local, mesh=fine, in_specs=placed, out_specs=P(ALL, None), check_vma=False)
```

```python
import functools
import jax
import jax.numpy as jnp
from jax import lax
from jax.experimental import pallas as pl
from jax.experimental.pallas import tpu as pltpu
from jax.sharding import Mesh, PartitionSpec as P

Y, Z, X, C = "y", "z", "x", "c"
ALL = (Y, Z, X, C)
XC = (X, C)
N_Y, N_Z, N_XC = 4, 8, 8
EXTRA = 128
VMEM = 20 << 20
VMEM_FFN = 52 << 20
FREE = pl.CostEstimate(flops=0, bytes_accessed=0, transcendentals=0)


def shift(block, axis, by):
    count = lax.axis_size(axis)
    return lax.ppermute(block, axis, [(i, (i + by) % count) for i in range(count)])


def after(value, *others):
    return lax.optimization_barrier((value, *others))[0]


def codes_kernel(mask_ref, tokens_ref, own_ref, other_ref, out_ref):
    count, width = tokens_ref.shape
    top = own_ref.shape[0] // 2
    experts = N_Z * N_XC
    slot = lax.broadcasted_iota(jnp.int32, (count, experts), 1)
    own = lax.broadcasted_iota(jnp.int32, (1, experts), 1)
    mask = jnp.concatenate([mask_ref[...], mask_ref[...]], axis=1)
    holder = jnp.where(mask == 1, own ^ (experts // 2), own).astype(jnp.float32)
    row = lax.broadcasted_iota(jnp.int32, (count, count), 0)
    earlier = (lax.broadcasted_iota(jnp.int32, (count, count), 1) < row).astype(jnp.bfloat16)
    lane = lax.broadcasted_iota(jnp.int32, (count, EXTRA), 1)
    out = jnp.zeros((count, EXTRA), jnp.float32)
    for ref, first in ((own_ref, 0), (other_ref, EXTRA // 2)):
        pairs = ref[...].T
        ids = pairs[:, :top].astype(jnp.int32)
        hits = [(ids[:, k : k + 1] == slot).astype(jnp.float32) for k in range(top)]
        chosen = functools.reduce(lambda p, q: p + q, hits)
        before = dot(earlier, chosen.astype(jnp.bfloat16))
        for k in range(top):
            out = jnp.where(lane == first + k, jnp.sum(hits[k] * holder, axis=1, keepdims=True), out)
            out = jnp.where(lane == first + top + k, jnp.sum(hits[k] * before, axis=1, keepdims=True), out)
            out = jnp.where(lane == first + 2 * top + k, pairs[:, top + k : top + k + 1], out)
    out_ref[:, :width] = tokens_ref[...]
    out_ref[:, width:] = out.astype(out_ref.dtype)


def with_codes(mask, tokens, own, other):
    return pl.pallas_call(
        codes_kernel,
        out_shape=jax.ShapeDtypeStruct((tokens.shape[0], tokens.shape[1] + EXTRA), jnp.bfloat16),
        cost_estimate=FREE,
    )(mask[None], tokens, own, other)


def rows_of(held_by, rank, token, per_z, capacity, z):
    held_by = held_by.astype(jnp.int32)
    row = ((held_by & (N_XC - 1)) * N_Z + token // per_z) * capacity + rank.astype(jnp.int32)
    return jnp.where(held_by // N_XC == z, row, -1)


def picks_kernel(first, top, capacity, z_ref, extra_ref, out_ref):
    across = extra_ref[...].astype(jnp.float32).T[first : first + 2 * top]
    count = across.shape[1]
    token = lax.broadcasted_iota(jnp.int32, (top, count), 1)
    row = rows_of(across[:top], across[top:], token, count // N_Z, capacity, z_ref[0])
    slot = lax.broadcasted_iota(jnp.int32, out_ref.shape, 0)
    hit = jnp.zeros(out_ref.shape, jnp.float32)
    for k in range(top):
        hit = jnp.where(row[k : k + 1] == slot, 1.0, hit)
    out_ref[...] = hit.astype(out_ref.dtype)


def mixes_kernel(first, top, capacity, z_ref, extra_ref, out_ref):
    values = extra_ref[:, first : first + 3 * top].astype(jnp.float32)
    count = values.shape[0]
    token = lax.broadcasted_iota(jnp.int32, (count, top), 0)
    row = rows_of(values[:, :top], values[:, top : 2 * top], token, count // N_Z, capacity, z_ref[0])
    slot = lax.broadcasted_iota(jnp.int32, out_ref.shape, 1)
    total = jnp.zeros(out_ref.shape, jnp.float32)
    for k in range(top):
        total = jnp.where(row[:, k : k + 1] == slot, values[:, 2 * top + k : 2 * top + k + 1], total)
    out_ref[...] = total.astype(out_ref.dtype)


def matrix(kernel, gathered, first, top, capacity, shape):
    count, width = gathered.shape
    return pl.pallas_call(
        functools.partial(kernel, first, top, capacity),
        grid=(1,),
        in_specs=[
            pl.BlockSpec(memory_space=pltpu.SMEM),
            pl.BlockSpec((count, EXTRA), lambda j: (0, width // EXTRA - 1)),
        ],
        out_specs=pl.BlockSpec(shape, lambda j: (0, 0)),
        out_shape=jax.ShapeDtypeStruct(shape, jnp.bfloat16),
        compiler_params=pltpu.CompilerParams(vmem_limit_bytes=VMEM),
        cost_estimate=FREE,
    )(lax.axis_index(Z).astype(jnp.int32)[None], gathered)


def apply_kernel(matrix_ref, value_ref, out_ref):
    out_ref[...] = dot(matrix_ref[...], value_ref[...]).astype(out_ref.dtype)


def apply(matrix, value, first, width, tile):
    rows, inner = matrix.shape
    at = first // tile
    return pl.pallas_call(
        apply_kernel,
        grid=(width // tile,),
        in_specs=[pl.BlockSpec((rows, inner), lambda j: (0, 0)), pl.BlockSpec((inner, tile), lambda j: (0, j + at))],
        out_specs=pl.BlockSpec((rows, tile), lambda j: (0, j)),
        out_shape=jax.ShapeDtypeStruct((rows, width), jnp.bfloat16),
        compiler_params=pltpu.CompilerParams(vmem_limit_bytes=VMEM),
        cost_estimate=FREE,
    )(matrix, value)


def sides_kernel(bounds, gate_ref, up_ref, *out_refs):
    units = gate_ref.shape[1]
    third, half = units // 3, units // 2
    gate, up = gate_ref[...], up_ref[...]
    low = jnp.concatenate([gate[:, :third], up[:, :third], gate[:, third:half], up[:, third:half]], axis=1)
    high = jnp.concatenate(
        [gate[:, units - third :], up[:, units - third :], gate[:, half : units - third], up[:, half : units - third]], axis=1
    )
    step = pl.program_id(0)
    for i, (first, last) in enumerate(zip(bounds, bounds[1:])):

        @pl.when((step >= first) & (step < last))
        def _():
            out_refs[2 * i][...] = low
            out_refs[2 * i + 1][...] = high


def sides(gate, up, bounds, tile):
    rows, units = gate.shape
    steps = [bound // tile for bound in bounds]

    def spec(first, last):
        return pl.BlockSpec((tile, units), lambda j: (jnp.clip(j - first, 0, last - first - 1), 0))

    ranges = [r for r in zip(bounds, bounds[1:]) for _ in range(2)]
    outs = pl.pallas_call(
        functools.partial(sides_kernel, steps),
        grid=(rows // tile,),
        in_specs=[pl.BlockSpec((tile, units), lambda j: (j, 0))] * 2,
        out_specs=[spec(first // tile, last // tile) for first, last in ranges],
        out_shape=[jax.ShapeDtypeStruct((last - first, units), gate.dtype) for first, last in ranges],
        compiler_params=pltpu.CompilerParams(vmem_limit_bytes=VMEM),
        cost_estimate=FREE,
    )(gate, up)
    return list(zip(outs[::2], outs[1::2]))


def ffn_kernel(moves, has_add, rows_ref, gate_ref, up_ref, *refs):
    side_refs, act_ref = refs[:6], refs[6]
    out_ref, low_ref, high_ref, weights, sems = refs[6 + has_add :]
    step = pl.program_id(0)
    third = gate_ref.shape[1]
    sixth = third // 2
    first_two = 2 * third
    copies = [
        pltpu.make_async_copy(
            side_refs[2 * i + j].at[pl.ds(source, count)], buffer.at[pl.ds(target, count)], sems.at[2 * i + j]
        )
        for i, source, target, count in moves
        for j, buffer in enumerate((low_ref, high_ref))
    ]

    @pl.when(step == 0)
    def _():
        for copy in copies:
            copy.start()

    @pl.when(step < 3)
    def _():
        weights[:, :third] = gate_ref[...]
        weights[:, third:] = up_ref[...]

    @pl.when(step == 3)
    def _():
        for copy in copies:
            copy.wait()
        weights[...] = low_ref[:, :first_two]

    @pl.when(step == 4)
    def _():
        low, high = low_ref[:, first_two:], high_ref[:, first_two:]
        weights[...] = jnp.concatenate([low[:, :sixth], high[:, :sixth], low[:, sixth:], high[:, sixth:]], axis=1)

    @pl.when(step == 5)
    def _():
        weights[...] = high_ref[:, :first_two]

    act = dot(rows_ref[...], weights[...])
    if has_add:
        act = act + act_ref[...]
        act = jax.nn.silu(act[:, :third]) * act[:, third:]
    out_ref[...] = act.astype(out_ref.dtype)


def ffn(rows, first, gate, up, side_weights, bounds, act=None):
    count, inner = rows.shape
    units = gate.shape[1]
    third = units // 3
    last = first + inner
    moves = []
    for i, (low, high) in enumerate(zip(bounds, bounds[1:])):
        start, stop = max(low, first), min(high, last)
        if start < stop:
            moves.append((i, start - low, start - first, stop - start))
    has_add = act is not None
    columns, dtype = (third, jnp.bfloat16) if has_add else (2 * third, jnp.float32)
    weight = pl.BlockSpec((inner, third), lambda j: (first // inner, jnp.minimum(j, 2)))
    return pl.pallas_call(
        functools.partial(ffn_kernel, moves, has_add),
        grid=(6,),
        in_specs=[pl.BlockSpec((count, inner), lambda j: (0, 0)), weight, weight]
        + [pl.BlockSpec(memory_space=pltpu.HBM)] * 6
        + [pl.BlockSpec((count, 2 * third), lambda j: (0, j))] * has_add,
        out_specs=pl.BlockSpec((count, columns), lambda j: (0, j)),
        out_shape=jax.ShapeDtypeStruct((count, 6 * columns), dtype),
        scratch_shapes=[
            pltpu.VMEM((inner, units), gate.dtype),
            pltpu.VMEM((inner, units), gate.dtype),
            pltpu.VMEM((inner, 2 * third), gate.dtype),
            pltpu.SemaphoreType.DMA((6,)),
        ],
        compiler_params=pltpu.CompilerParams(vmem_limit_bytes=VMEM_FFN),
        cost_estimate=pl.CostEstimate(flops=12 * count * inner * units, bytes_accessed=6 * inner * units, transcendentals=0),
    )(rows, gate, up, *side_weights, *([act] if has_add else []))


def down_kernel(has_add, hidden_ref, own_ref, low_ref, high_ref, *refs):
    weights = jnp.concatenate([own_ref[...], low_ref[...], high_ref[...]], axis=0)
    result = dot(hidden_ref[...], weights)
    if has_add:
        result = result + refs[0][...].astype(jnp.float32)
    refs[-1][...] = result.astype(refs[-1].dtype)


def down(hidden, own, low, high, first, width, tile, add=None):
    count, units = hidden.shape
    at = first // tile
    half = low.shape[0]
    extra = [] if add is None else [add]
    return pl.pallas_call(
        functools.partial(down_kernel, add is not None),
        grid=(width // tile,),
        in_specs=[
            pl.BlockSpec((count, units), lambda j: (0, 0)),
            pl.BlockSpec((own.shape[0], tile), lambda j: (0, j + at)),
            pl.BlockSpec((half, tile), lambda j: (0, j + at)),
            pl.BlockSpec((half, tile), lambda j: (0, j + at)),
        ]
        + [pl.BlockSpec((count, tile), lambda j: (0, j))] * len(extra),
        out_specs=pl.BlockSpec((count, tile), lambda j: (0, j)),
        out_shape=jax.ShapeDtypeStruct((count, width), jnp.bfloat16),
        compiler_params=pltpu.CompilerParams(vmem_limit_bytes=VMEM),
        cost_estimate=FREE,
    )(hidden, own, low, high, *extra)


def dot(a, b):
    return jnp.dot(a, b, preferred_element_type=jnp.float32)


def exchange(rows):
    parts = rows.reshape(N_XC, rows.shape[0] // N_XC, rows.shape[1])
    return lax.all_to_all(parts, XC, split_axis=0, concat_axis=0, tiled=True).reshape(rows.shape)


def local(tokens, expert_ids, gate_values, swap_mask, gate_weight, up_weight, down_weight):
    tok_count, width = tokens.shape
    top = expert_ids.shape[1]
    experts = N_Z * N_XC
    capacity = min(tok_count, tok_count * top // experts + 1)
    cut = width // 2
    tile = min(512, cut)
    back = width // 8 * 5
    rest = width - back
    w_gate, w_up, w_down = gate_weight[0], up_weight[0], down_weight[0]
    units = w_gate.shape[1]
    half = units // 2

    pairs = jnp.concatenate([expert_ids.T.astype(jnp.float32), gate_values.T], axis=0)
    down_parts = after((w_down[:half], w_down[half:]), pairs)
    pairs_other, *down_parts = lax.optimization_barrier((shift(pairs, Y, 2), *down_parts))
    own_tokens = with_codes(swap_mask, tokens, pairs, pairs_other)
    other_tokens = shift(after(tokens[:, :cut], own_tokens), Y, 2)

    def swap(parts):
        return shift(parts[0], Y, -1), shift(parts[1], Y, 1)

    bounds = [0, width // 16 * 6, width // 16 * 11, width]
    side_2, side_1, side_0 = sides(after(w_gate, own_tokens), w_up, bounds, width // 16)
    down_low, down_high = swap(down_parts)
    side_0 = swap(after(side_0, down_low, down_high, other_tokens))
    side_1 = swap(after(side_1, *side_0))
    side_2 = swap(after(side_2, *side_1))

    own_all = lax.all_gather(own_tokens, Z, axis=0, tiled=True)
    other_all = lax.all_gather(after(other_tokens, own_tokens), Z, axis=0, tiled=True)
    own_all = after(own_all, down_low, down_high)

    late_width = width - cut
    rows, count = N_XC * N_Z * capacity, N_Z * tok_count
    second = EXTRA // 2
    pick_own = matrix(picks_kernel, own_all, 0, top, capacity, (rows, count))
    late_rows = apply(pick_own, own_all, cut, late_width, tile)
    own_rows = apply(after(pick_own, late_rows), own_all, 0, cut, tile)
    own_late = exchange(after(late_rows, own_rows, *side_0))
    own_early = exchange(after(own_rows, own_late, *side_1))
    mix_own = matrix(mixes_kernel, after(own_all, own_rows), 0, top, capacity, (count, rows))
    pick_other = matrix(picks_kernel, after(own_all, mix_own), second, top, capacity, (rows, count))
    other_rows = apply(pick_other, other_all, 0, cut, tile)
    other_early = exchange(after(other_rows, own_early, *side_2))
    mix_other = matrix(mixes_kernel, after(own_all, other_rows), second, top, capacity, (count, rows))
    other_late = shift(after(own_late, *side_2), Y, 2)

    side_weights = (*side_2, *side_1, *side_0)

    def part(rows, first, act=None):
        return ffn(rows, first, w_gate, w_up, side_weights, bounds, act)

    early_down = (w_down, down_low, down_high, 0, back, tile)
    late_down = (w_down, down_low, down_high, back, rest, tile)
    hidden_own = part(own_early, 0, part(own_late, cut))
    own_out = down(hidden_own, *early_down)
    own_back = exchange(after(own_out, other_early))
    hidden_other = part(other_late, cut, part(other_early, 0))
    late_for_other = down(hidden_other, *late_down)
    late_from_other = shift(late_for_other, Y, 2)
    other_out = down(after(hidden_other, late_for_other), *early_down)

    own_mixed = apply(mix_own, after(own_back, other_out), 0, back, tile)
    own_sum = lax.psum_scatter(own_mixed, Z, scatter_dimension=0, tiled=True)
    other_back = exchange(other_out)
    other_mixed = apply(mix_other, other_back, 0, back, tile)
    other_sum = lax.psum_scatter(after(other_mixed, late_from_other, own_sum), Z, scatter_dimension=0, tiled=True)
    early_final = own_sum.astype(jnp.float32) + shift(other_sum, Y, 2).astype(jnp.float32)

    late_out = down(hidden_own, *late_down, late_from_other)
    late_back = exchange(after(late_out, other_mixed))
    late_final = lax.psum_scatter(apply(mix_own, late_back, 0, rest, tile), Z, scatter_dimension=0, tiled=True)
    result = jnp.pad(early_final.astype(jnp.bfloat16), ((0, 0), (0, rest)))
    return lax.dynamic_update_slice(result, late_final, (0, back))


def solution(mesh):
    fine = Mesh(mesh.devices.reshape(N_Y, N_Z, N_XC // 2, 2), ALL)
    experts = (Z, X, C)
    placed = (
        P(ALL, None),
        P(ALL, None),
        P(ALL, None),
        P(),
        P(experts, None, Y),
        P(experts, None, Y),
        P(experts, Y, None),
    )
    return jax.shard_map(local, mesh=fine, in_specs=placed, out_specs=P(ALL, None), check_vma=False)
```

```python
import functools
import jax
import jax.numpy as jnp
from jax import lax
from jax.experimental import pallas as pl
from jax.experimental.pallas import tpu as pltpu
from jax.sharding import Mesh, PartitionSpec as P

Y, Z, X, C = "y", "z", "x", "c"
ALL = (Y, Z, X, C)
XC = (X, C)
N_Y, N_Z, N_XC = 4, 8, 8
EXTRA = 128
VMEM = 20 << 20
VMEM_FFN = 52 << 20
FREE = pl.CostEstimate(flops=0, bytes_accessed=0, transcendentals=0)


def shift(block, axis, by):
    count = lax.axis_size(axis)
    return lax.ppermute(block, axis, [(i, (i + by) % count) for i in range(count)])


def after(value, *others):
    return lax.optimization_barrier((value, *others))[0]


def codes_kernel(mask_ref, tokens_ref, own_ref, other_ref, out_ref):
    count, width = tokens_ref.shape
    top = own_ref.shape[0] // 2
    experts = N_Z * N_XC
    slot = lax.broadcasted_iota(jnp.int32, (count, experts), 1)
    own = lax.broadcasted_iota(jnp.int32, (1, experts), 1)
    mask = jnp.concatenate([mask_ref[...], mask_ref[...]], axis=1)
    holder = jnp.where(mask == 1, own ^ (experts // 2), own).astype(jnp.float32)
    row = lax.broadcasted_iota(jnp.int32, (count, count), 0)
    earlier = (lax.broadcasted_iota(jnp.int32, (count, count), 1) < row).astype(jnp.bfloat16)
    lane = lax.broadcasted_iota(jnp.int32, (count, EXTRA), 1)
    out = jnp.zeros((count, EXTRA), jnp.float32)
    for ref, first in ((own_ref, 0), (other_ref, EXTRA // 2)):
        pairs = ref[...].T
        ids = pairs[:, :top].astype(jnp.int32)
        hits = [(ids[:, k : k + 1] == slot).astype(jnp.float32) for k in range(top)]
        chosen = functools.reduce(lambda p, q: p + q, hits)
        before = dot(earlier, chosen.astype(jnp.bfloat16))
        for k in range(top):
            out = jnp.where(lane == first + k, jnp.sum(hits[k] * holder, axis=1, keepdims=True), out)
            out = jnp.where(lane == first + top + k, jnp.sum(hits[k] * before, axis=1, keepdims=True), out)
            out = jnp.where(lane == first + 2 * top + k, pairs[:, top + k : top + k + 1], out)
    out_ref[:, :width] = tokens_ref[...]
    out_ref[:, width:] = out.astype(out_ref.dtype)


def with_codes(mask, tokens, own, other):
    return pl.pallas_call(
        codes_kernel,
        out_shape=jax.ShapeDtypeStruct((tokens.shape[0], tokens.shape[1] + EXTRA), jnp.bfloat16),
        cost_estimate=FREE,
    )(mask[None], tokens, own, other)


def rows_of(held_by, rank, token, per_z, capacity, z):
    held_by = held_by.astype(jnp.int32)
    row = ((held_by & (N_XC - 1)) * N_Z + token // per_z) * capacity + rank.astype(jnp.int32)
    return jnp.where(held_by // N_XC == z, row, -1)


def picks_kernel(first, top, capacity, z_ref, extra_ref, out_ref):
    across = extra_ref[...].astype(jnp.float32).T[first : first + 2 * top]
    count = across.shape[1]
    token = lax.broadcasted_iota(jnp.int32, (top, count), 1)
    row = rows_of(across[:top], across[top:], token, count // N_Z, capacity, z_ref[0])
    slot = lax.broadcasted_iota(jnp.int32, out_ref.shape, 0)
    hit = jnp.zeros(out_ref.shape, jnp.float32)
    for k in range(top):
        hit = jnp.where(row[k : k + 1] == slot, 1.0, hit)
    out_ref[...] = hit.astype(out_ref.dtype)


def mixes_kernel(first, top, capacity, z_ref, extra_ref, out_ref):
    values = extra_ref[:, first : first + 3 * top].astype(jnp.float32)
    count = values.shape[0]
    token = lax.broadcasted_iota(jnp.int32, (count, top), 0)
    row = rows_of(values[:, :top], values[:, top : 2 * top], token, count // N_Z, capacity, z_ref[0])
    slot = lax.broadcasted_iota(jnp.int32, out_ref.shape, 1)
    total = jnp.zeros(out_ref.shape, jnp.float32)
    for k in range(top):
        total = jnp.where(row[:, k : k + 1] == slot, values[:, 2 * top + k : 2 * top + k + 1], total)
    out_ref[...] = total.astype(out_ref.dtype)


def matrix(kernel, gathered, first, top, capacity, shape):
    count, width = gathered.shape
    return pl.pallas_call(
        functools.partial(kernel, first, top, capacity),
        grid=(1,),
        in_specs=[
            pl.BlockSpec(memory_space=pltpu.SMEM),
            pl.BlockSpec((count, EXTRA), lambda j: (0, width // EXTRA - 1)),
        ],
        out_specs=pl.BlockSpec(shape, lambda j: (0, 0)),
        out_shape=jax.ShapeDtypeStruct(shape, jnp.bfloat16),
        compiler_params=pltpu.CompilerParams(vmem_limit_bytes=VMEM),
        cost_estimate=FREE,
    )(lax.axis_index(Z).astype(jnp.int32)[None], gathered)


def apply_kernel(matrix_ref, value_ref, out_ref):
    out_ref[...] = dot(matrix_ref[...], value_ref[...]).astype(out_ref.dtype)


def apply(matrix, value, first, width, tile):
    rows, inner = matrix.shape
    at = first // tile
    return pl.pallas_call(
        apply_kernel,
        grid=(width // tile,),
        in_specs=[pl.BlockSpec((rows, inner), lambda j: (0, 0)), pl.BlockSpec((inner, tile), lambda j: (0, j + at))],
        out_specs=pl.BlockSpec((rows, tile), lambda j: (0, j)),
        out_shape=jax.ShapeDtypeStruct((rows, width), jnp.bfloat16),
        compiler_params=pltpu.CompilerParams(vmem_limit_bytes=VMEM),
        cost_estimate=FREE,
    )(matrix, value)


def sides_kernel(bounds, gate_ref, up_ref, *out_refs):
    units = gate_ref.shape[1]
    third, half = units // 3, units // 2
    gate, up = gate_ref[...], up_ref[...]
    low = jnp.concatenate([gate[:, :third], up[:, :third], gate[:, third:half], up[:, third:half]], axis=1)
    high = jnp.concatenate(
        [gate[:, units - third :], up[:, units - third :], gate[:, half : units - third], up[:, half : units - third]], axis=1
    )
    step = pl.program_id(0)
    for i, (first, last) in enumerate(zip(bounds, bounds[1:])):

        @pl.when((step >= first) & (step < last))
        def _():
            out_refs[2 * i][...] = low
            out_refs[2 * i + 1][...] = high


def sides(gate, up, bounds, tile):
    rows, units = gate.shape
    steps = [bound // tile for bound in bounds]

    def spec(first, last):
        return pl.BlockSpec((tile, units), lambda j: (jnp.clip(j - first, 0, last - first - 1), 0))

    ranges = [r for r in zip(bounds, bounds[1:]) for _ in range(2)]
    outs = pl.pallas_call(
        functools.partial(sides_kernel, steps),
        grid=(rows // tile,),
        in_specs=[pl.BlockSpec((tile, units), lambda j: (j, 0))] * 2,
        out_specs=[spec(first // tile, last // tile) for first, last in ranges],
        out_shape=[jax.ShapeDtypeStruct((last - first, units), gate.dtype) for first, last in ranges],
        compiler_params=pltpu.CompilerParams(vmem_limit_bytes=VMEM),
        cost_estimate=FREE,
    )(gate, up)
    return list(zip(outs[::2], outs[1::2]))


def ffn_kernel(moves, has_add, rows_ref, gate_ref, up_ref, *refs):
    side_refs, act_ref = refs[:6], refs[6]
    out_ref, low_ref, high_ref, weights, sems = refs[6 + has_add :]
    step = pl.program_id(0)
    third = gate_ref.shape[1]
    sixth = third // 2
    first_two = 2 * third
    copies = [
        pltpu.make_async_copy(
            side_refs[2 * i + j].at[pl.ds(source, count)], buffer.at[pl.ds(target, count)], sems.at[2 * i + j]
        )
        for i, source, target, count in moves
        for j, buffer in enumerate((low_ref, high_ref))
    ]

    @pl.when(step == 0)
    def _():
        for copy in copies:
            copy.start()

    @pl.when(step < 3)
    def _():
        weights[:, :third] = gate_ref[...]
        weights[:, third:] = up_ref[...]

    @pl.when(step == 3)
    def _():
        for copy in copies:
            copy.wait()
        weights[...] = low_ref[:, :first_two]

    @pl.when(step == 4)
    def _():
        low, high = low_ref[:, first_two:], high_ref[:, first_two:]
        weights[...] = jnp.concatenate([low[:, :sixth], high[:, :sixth], low[:, sixth:], high[:, sixth:]], axis=1)

    @pl.when(step == 5)
    def _():
        weights[...] = high_ref[:, :first_two]

    act = dot(rows_ref[...], weights[...])
    if has_add:
        act = act + act_ref[...]
        act = jax.nn.silu(act[:, :third]) * act[:, third:]
    out_ref[...] = act.astype(out_ref.dtype)


def ffn(rows, first, gate, up, side_weights, bounds, act=None):
    count, inner = rows.shape
    units = gate.shape[1]
    third = units // 3
    last = first + inner
    moves = []
    for i, (low, high) in enumerate(zip(bounds, bounds[1:])):
        start, stop = max(low, first), min(high, last)
        if start < stop:
            moves.append((i, start - low, start - first, stop - start))
    has_add = act is not None
    columns, dtype = (third, jnp.bfloat16) if has_add else (2 * third, jnp.float32)
    weight = pl.BlockSpec((inner, third), lambda j: (first // inner, jnp.minimum(j, 2)))
    return pl.pallas_call(
        functools.partial(ffn_kernel, moves, has_add),
        grid=(6,),
        in_specs=[pl.BlockSpec((count, inner), lambda j: (0, 0)), weight, weight]
        + [pl.BlockSpec(memory_space=pltpu.HBM)] * 6
        + [pl.BlockSpec((count, 2 * third), lambda j: (0, j))] * has_add,
        out_specs=pl.BlockSpec((count, columns), lambda j: (0, j)),
        out_shape=jax.ShapeDtypeStruct((count, 6 * columns), dtype),
        scratch_shapes=[
            pltpu.VMEM((inner, units), gate.dtype),
            pltpu.VMEM((inner, units), gate.dtype),
            pltpu.VMEM((inner, 2 * third), gate.dtype),
            pltpu.SemaphoreType.DMA((6,)),
        ],
        compiler_params=pltpu.CompilerParams(vmem_limit_bytes=VMEM_FFN),
        cost_estimate=pl.CostEstimate(flops=12 * count * inner * units, bytes_accessed=6 * inner * units, transcendentals=0),
    )(rows, gate, up, *side_weights, *([act] if has_add else []))


def down_kernel(has_add, hidden_ref, own_ref, low_ref, high_ref, *refs):
    weights = jnp.concatenate([own_ref[...], low_ref[...], high_ref[...]], axis=0)
    result = dot(hidden_ref[...], weights)
    if has_add:
        result = result + refs[0][...].astype(jnp.float32)
    refs[-1][...] = result.astype(refs[-1].dtype)


def down(hidden, own, low, high, first, width, tile, add=None):
    count, units = hidden.shape
    at = first // tile
    half = low.shape[0]
    extra = [] if add is None else [add]
    return pl.pallas_call(
        functools.partial(down_kernel, add is not None),
        grid=(width // tile,),
        in_specs=[
            pl.BlockSpec((count, units), lambda j: (0, 0)),
            pl.BlockSpec((own.shape[0], tile), lambda j: (0, j + at)),
            pl.BlockSpec((half, tile), lambda j: (0, j + at)),
            pl.BlockSpec((half, tile), lambda j: (0, j + at)),
        ]
        + [pl.BlockSpec((count, tile), lambda j: (0, j))] * len(extra),
        out_specs=pl.BlockSpec((count, tile), lambda j: (0, j)),
        out_shape=jax.ShapeDtypeStruct((count, width), jnp.bfloat16),
        compiler_params=pltpu.CompilerParams(vmem_limit_bytes=VMEM),
        cost_estimate=FREE,
    )(hidden, own, low, high, *extra)


def dot(a, b):
    return jnp.dot(a, b, preferred_element_type=jnp.float32)


def exchange(rows):
    parts = rows.reshape(N_XC, rows.shape[0] // N_XC, rows.shape[1])
    return lax.all_to_all(parts, XC, split_axis=0, concat_axis=0, tiled=True).reshape(rows.shape)


def local(tokens, expert_ids, gate_values, swap_mask, gate_weight, up_weight, down_weight):
    tok_count, width = tokens.shape
    top = expert_ids.shape[1]
    experts = N_Z * N_XC
    capacity = min(tok_count, tok_count * top // experts + 1)
    cut = width // 2
    tile = min(512, cut)
    back = width // 8 * 5
    rest = width - back
    w_gate, w_up, w_down = gate_weight[0], up_weight[0], down_weight[0]
    units = w_gate.shape[1]
    half = units // 2

    pairs = jnp.concatenate([expert_ids.T.astype(jnp.float32), gate_values.T], axis=0)
    down_parts = after((w_down[:half], w_down[half:]), pairs)
    pairs_other, *down_parts = lax.optimization_barrier((shift(pairs, Y, 2), *down_parts))
    own_tokens = with_codes(swap_mask, tokens, pairs, pairs_other)
    other_tokens = shift(after(tokens[:, :cut], own_tokens), Y, 2)

    def swap(parts):
        return shift(parts[0], Y, -1), shift(parts[1], Y, 1)

    bounds = [0, width // 16 * 5, width // 16 * 11, width]
    side_2, side_1, side_0 = sides(after(w_gate, own_tokens), w_up, bounds, width // 16)
    down_low, down_high = swap(down_parts)
    side_0 = swap(after(side_0, down_low, down_high, other_tokens))
    side_1 = swap(after(side_1, *side_0))
    side_2 = swap(after(side_2, *side_1))

    own_all = lax.all_gather(own_tokens, Z, axis=0, tiled=True)
    other_all = lax.all_gather(after(other_tokens, own_tokens), Z, axis=0, tiled=True)
    own_all = after(own_all, down_low, down_high)

    late_width = width - cut
    rows, count = N_XC * N_Z * capacity, N_Z * tok_count
    second = EXTRA // 2
    pick_own = matrix(picks_kernel, own_all, 0, top, capacity, (rows, count))
    late_rows = apply(pick_own, own_all, cut, late_width, tile)
    own_rows = apply(after(pick_own, late_rows), own_all, 0, cut, tile)
    own_late = exchange(after(late_rows, own_rows, *side_0))
    own_early = exchange(after(own_rows, own_late, *side_1))
    mix_own = matrix(mixes_kernel, after(own_all, own_rows), 0, top, capacity, (count, rows))
    pick_other = matrix(picks_kernel, after(own_all, mix_own), second, top, capacity, (rows, count))
    other_rows = apply(pick_other, other_all, 0, cut, tile)
    other_early = exchange(after(other_rows, own_early, *side_2))
    mix_other = matrix(mixes_kernel, after(own_all, other_rows), second, top, capacity, (count, rows))
    other_late = shift(after(own_late, *side_2), Y, 2)

    side_weights = (*side_2, *side_1, *side_0)

    def part(rows, first, act=None):
        return ffn(rows, first, w_gate, w_up, side_weights, bounds, act)

    early_down = (w_down, down_low, down_high, 0, back, tile)
    late_down = (w_down, down_low, down_high, back, rest, tile)
    hidden_own = part(own_early, 0, part(own_late, cut))
    own_out = down(hidden_own, *early_down)
    own_back = exchange(after(own_out, other_early))
    hidden_other = part(other_late, cut, part(other_early, 0))
    late_for_other = down(hidden_other, *late_down)
    late_from_other = shift(late_for_other, Y, 2)
    other_out = down(after(hidden_other, late_for_other), *early_down)

    own_mixed = apply(mix_own, after(own_back, other_out), 0, back, tile)
    own_sum = lax.psum_scatter(own_mixed, Z, scatter_dimension=0, tiled=True)
    other_back = exchange(other_out)
    other_mixed = apply(mix_other, other_back, 0, back, tile)
    other_sum = lax.psum_scatter(after(other_mixed, late_from_other, own_sum), Z, scatter_dimension=0, tiled=True)
    early_final = own_sum.astype(jnp.float32) + shift(other_sum, Y, 2).astype(jnp.float32)

    late_out = down(hidden_own, *late_down, late_from_other)
    late_back = exchange(after(late_out, other_mixed))
    late_final = lax.psum_scatter(apply(mix_own, late_back, 0, rest, tile), Z, scatter_dimension=0, tiled=True)
    result = jnp.pad(early_final.astype(jnp.bfloat16), ((0, 0), (0, rest)))
    return lax.dynamic_update_slice(result, late_final, (0, back))


def solution(mesh):
    fine = Mesh(mesh.devices.reshape(N_Y, N_Z, N_XC // 2, 2), ALL)
    experts = (Z, X, C)
    placed = (
        P(ALL, None),
        P(ALL, None),
        P(ALL, None),
        P(),
        P(experts, None, Y),
        P(experts, None, Y),
        P(experts, Y, None),
    )
    return jax.shard_map(local, mesh=fine, in_specs=placed, out_specs=P(ALL, None), check_vma=False)
```
